256 devices in a mesh: dp: 8 (over y, core), expert: 32 (over z, x).
Axes of the slice: x: 4, y: 4, z: 8, core: 2. Of those that a mesh axis runs over, the one named last changes fastest.
Arguments:
- tokens: bfloat16 [32768, 1024], P(('dp', 'expert')), may hold values from -6 to 6
- cotangent: bfloat16 [32768, 1024], P(('dp', 'expert')), may hold values from -12 to 12
- gates: float32 [32768, 8], P(('dp', 'expert')), may hold values from 0.05 to 1
- routes: int32 [32768, 8], P(('dp', 'expert')), may hold values from 0 to 31, all different within a row; in each aligned block of 128 rows (0 to 127, 128 to 255, ...) at most 48 rows name the same one
- old_place: int32 [8, 32], P('dp'), may hold values from 0 to 15, as said below
- new_place: int32 [8, 32], P('dp'), may hold values from 0 to 15, as said below
- up_weight: bfloat16 [8, 32, 1024, 384], P('dp', 'expert'), as said below
- down_weight: bfloat16 [8, 32, 1024, 384], P('dp', 'expert'), as said below
- first_moment: float32 [8, 32, 2, 1024, 384], P('dp', 'expert'), as said below
- second_moment: float32 [8, 32, 2, 1024, 384], P('dp', 'expert'), as said below
Outputs:
- layer_out: bfloat16 [32768, 1024], P(('dp', 'expert'))
- token_grad: bfloat16 [32768, 1024], P(('dp', 'expert'))
- update_dir: bfloat16 [8, 32, 2, 1024, 384], P('dp', 'expert')
The draws below stay inside these ranges and needn't reach their ends.
Inputs may be any that keep to these rules, and one draw needn't show every extreme that they name: `routes`: within the rows of one device no slot is named more than 48 times, a bound that some block reaches; the 8 slots of a row differ. `old_place`: every expert appears in every row, some more than once. `new_place`: every expert appears in every row, some more than once. `up_weight`: slots that hold the same expert in old_place, in any group, hold equal entries. `down_weight`: slots that hold the same expert in old_place, in any group, hold equal entries. `first_moment`: slots that hold the same expert in old_place, in any group, hold equal entries. `second_moment`: slots that hold the same expert in old_place, in any group, hold equal entries; all positive.
All inputs are finite; a program needn't handle non-finite values.
Results may differ from the reference program's by a relative error of at most 0.0068.
Values may be sent and summed in bfloat16 or wider, within the bound.
No kernel may reach another device: no remote copies, remote signals or barrier semaphores. Data moves between devices by JAX's collectives and lax.ppermute only.
A program may use at most 128 MiB of HBM per device.

```python
import math
from functools import partial
import jax
import jax.numpy as jnp
import numpy as np
from jax import lax

D = 1024
H = 384
TOPK = 8
TOK_DEV = 128
EXPERTS = 16
CAP = 48
TOKENS = 32768
N_DP = 8
N_EXPERT = 32


def one_placement(key):
    first_key, second_key, third_key = jax.random.split(key, 3)
    shuffled = jax.random.permutation(first_key, EXPERTS).astype(jnp.int32)
    popular = max(1, EXPERTS // 4)
    repeats = shuffled[jax.random.randint(second_key, (N_EXPERT - EXPERTS,), 0, popular)]
    joined_row = jnp.concatenate([shuffled, repeats])
    return joined_row[jax.random.permutation(third_key, N_EXPERT)].astype(jnp.int32)


def placement_rows(key):
    key = jax.random.fold_in(key, 101)
    row_keys = jax.random.split(key, N_DP)
    return jax.vmap(one_placement)(row_keys)


def draw_old_place(key, part):
    return placement_rows(key)


def draw_new_place(key, part):
    key = jax.random.fold_in(key, 202)
    return placement_rows(key)


def draw_up_weight(key, part):
    old_rows = placement_rows(key)
    key = jax.random.fold_in(key, 3)
    table = jnp.clip(jax.random.normal(key, (EXPERTS, D, H), jnp.float32), -6.0, 6.0)
    table = table / math.sqrt(D)
    return table[old_rows].astype(jnp.bfloat16)


def draw_down_weight(key, part):
    old_rows = placement_rows(key)
    key = jax.random.fold_in(key, 4)
    table = jnp.clip(jax.random.normal(key, (EXPERTS, D, H), jnp.float32), -6.0, 6.0)
    table = table / math.sqrt(H)
    return table[old_rows].astype(jnp.bfloat16)


def draw_first_moment(key, part):
    old_rows = placement_rows(key)
    key = jax.random.fold_in(key, 5)
    table = 8.0 * jnp.clip(jax.random.normal(key, (EXPERTS, 2, D, H), jnp.float32), -5.0, 5.0)
    return table[old_rows].astype(jnp.float32)


def draw_second_moment(key, part):
    old_rows = placement_rows(key)
    key = jax.random.fold_in(key, 6)
    table = jnp.exp(jax.random.uniform(key, (EXPERTS, 2, D, H), jnp.float32, math.log(16.0), math.log(256.0)))
    return table[old_rows].astype(jnp.float32)


def level_of(key, dims, cuts, least, largest):
    factor_of = 1.0
    for dim, shards_of in cuts:
        steps = jax.random.uniform(jax.random.fold_in(jax.random.fold_in(key, 6), dim), (shards_of,), jnp.float32, least / len(cuts), largest / len(cuts))
        factor_of = factor_of * jnp.repeat(jnp.exp(steps), dims[dim] // shards_of).reshape((-1,) + (1,) * (len(dims) - 1 - dim))
    return factor_of


def shared_out(own_key, own, number, rows, amount, top, reach, skew):
    order = jax.random.permutation(own_key, amount)
    crowded, common = portions_of(amount, rows * top, reach, skew, True), portions_of(amount, rows * top, reach, skew, False)
    places = jnp.arange(amount)

    def named(tallies, turn):
        used = int((tallies > 0).sum())
        fixed = max(1, used // 4)
        moved = fixed + (places - fixed + turn * (used - fixed)) % max(1, amount - fixed)
        return jnp.zeros((amount,), jnp.int32).at[order[jnp.where(places < fixed, places, moved)]].set(jnp.asarray(tallies, jnp.int32))

    tallies = jnp.where(number % 4 == 0, named(crowded, number // 4), named(common, number - number // 4 - 1))
    mixed = jax.random.permutation(jax.random.fold_in(own, 3), amount)
    source_of, sink = mixed[0:amount // 2 * 2:2], mixed[1:amount // 2 * 2:2]
    room = jnp.minimum(tallies[source_of] - 1, reach - tallies[sink]) // 2
    room = jnp.where((source_of == order[0]) | (sink == order[0]) | (tallies[sink] == 0), 0, jnp.maximum(room, 0))
    moved = jax.random.randint(jax.random.fold_in(own, 4), (amount // 2,), 0, 1 << 20) % (room + 1)
    tallies = tallies.at[source_of].add(-moved).at[sink].add(moved)
    labels = jnp.searchsorted(jnp.cumsum(tallies), jnp.arange(rows * top), side="right").astype(jnp.int32)
    grid = labels.reshape(top, rows).T
    grid = grid[jax.random.permutation(jax.random.fold_in(own, 1), rows)]
    turn = jax.random.randint(jax.random.fold_in(own, 2), (rows, 1), 0, top)
    return jnp.take_along_axis(grid, (jnp.arange(top)[None, :] + turn) % top, axis=1)


def portions_of(count, total, limit, skew, full):
    portions = [(1 << 20) // math.isqrt(rank ** skew) + 1 for rank in range(1, count + 1)]
    largest = limit if full else min(limit, max(-(-total // count), total * portions[0] // sum(portions)))
    least = 1 if total - largest >= count - 1 else 0
    given, rest = [largest] + [least] * (count - 1), total - largest - least * (count - 1)
    while rest > 0:
        free = [i for i in range(1, count) if given[i] < largest] or [i for i in range(1, count) if given[i] < limit]
        pool, budget = sum([portions[i] for i in free]), rest
        for i in free:
            addition = min(limit - given[i], max(1, budget * portions[i] // pool), rest)
            given[i] = given[i] + addition
            rest = rest - addition
    return np.array(given)


def normal_values(own_key, shape, spread, most, pieces=(), held_as=jnp.bfloat16):
    entries = jax.random.normal(own_key, shape, jnp.float32) * spread
    if len(pieces) > 0:
        entries = level_of(own_key, shape, pieces, -0.22, 0.18) * entries
    return jnp.clip(entries, min=-most, max=most).astype(held_as)


def setup_inputs(seed: int = 0) -> dict:
    arg_keys = jax.random.split(jax.random.key(seed), 11)
    tokens = normal_values(arg_keys[0], (TOKENS, D), 1.0, 6.0, ((0, 256),))
    cotangent = normal_values(arg_keys[1], (TOKENS, D), 2.0, 12.0, ((0, 256),))
    gates = jnp.clip(jnp.exp(math.log(1.0) - 2.9957323 * jax.random.uniform(arg_keys[2], (TOKENS, TOPK), jnp.float32) ** level_of(arg_keys[2], (TOKENS, TOPK), ((0, 256),), -0.2, 0.2)), 0.05, 1.0)
    routes_keys = jax.random.split(jax.random.fold_in(arg_keys[3], 1), TOKENS // TOK_DEV)
    routes_turns = jax.random.permutation(jax.random.fold_in(arg_keys[3], 3), TOKENS // TOK_DEV)
    routes = jax.vmap(lambda own, number: shared_out(jax.random.fold_in(arg_keys[3], 2), own, number, TOK_DEV, N_EXPERT, TOPK, CAP, 2))(routes_keys, routes_turns).reshape((TOKENS, TOPK))
    old_place = draw_old_place(jax.random.fold_in(arg_keys[10], 71), 0)
    new_place = draw_new_place(jax.random.fold_in(arg_keys[10], 71), 0)
    up_weight = draw_up_weight(jax.random.fold_in(arg_keys[10], 71), 0)
    down_weight = draw_down_weight(jax.random.fold_in(arg_keys[10], 71), 0)
    first_moment = draw_first_moment(jax.random.fold_in(arg_keys[10], 71), 0)
    second_moment = draw_second_moment(jax.random.fold_in(arg_keys[10], 71), 0)
    return dict(tokens=tokens, cotangent=cotangent, gates=gates, routes=routes, old_place=old_place, new_place=new_place, up_weight=up_weight, down_weight=down_weight, first_moment=first_moment, second_moment=second_moment)


BETA_ONE = 0.9
BETA_TWO = 0.95
EPSILON = 1e-08

def slot_targets(routes, slot_count, capacity):
    routes_flat = routes.reshape(-1).astype(jnp.int32)
    one_hot = (routes_flat[:, None] == jnp.arange(slot_count, dtype=jnp.int32)[None, :]).astype(jnp.int32)
    earlier = (jnp.cumsum(one_hot, axis=0) - one_hot).astype(jnp.int32)
    placed = lax.optimization_barrier(jnp.sum(earlier * one_hot, axis=1)).astype(jnp.int32)
    return (routes_flat * capacity + placed).astype(jnp.int32)

def fill_slots(targets, slot_total):
    numbers = jnp.arange(1, targets.shape[0] + 1, dtype=jnp.int32)
    return jnp.zeros((slot_total,), jnp.int32).at[targets].set(numbers)

def first_slots(old_ids, wanted):
    slot_total = old_ids.shape[0]
    positions = jnp.arange(slot_total, dtype=jnp.int32)
    matches = old_ids[None, :] == wanted[:, None]
    return lax.optimization_barrier(jnp.min(jnp.where(matches, positions[None, :], slot_total), axis=1)).astype(jnp.int32)

def silu_slope(preact):
    sigmoid_of = jax.nn.sigmoid(preact)
    return sigmoid_of * (1.0 + preact * (1.0 - sigmoid_of))

def adam_direction(expert_grads, first, second):
    new_first = BETA_ONE * first + (1.0 - BETA_ONE) * expert_grads
    new_second = BETA_TWO * second + (1.0 - BETA_TWO) * expert_grads * expert_grads
    return (new_first / (jnp.sqrt(new_second) + EPSILON)).astype(jnp.bfloat16)

def expert_apply(slot_data):
    slot_rows, out_grad, slab_up, slab_down = slot_data
    preact = jnp.dot(slot_rows, slab_up, preferred_element_type=jnp.float32)
    activated = jax.nn.silu(preact).astype(jnp.bfloat16)
    expert_out = jnp.dot(activated, slab_down.T, preferred_element_type=jnp.float32).astype(jnp.bfloat16)
    hidden_grad = jnp.dot(out_grad, slab_down, preferred_element_type=jnp.float32)
    pre_grad = (hidden_grad * silu_slope(preact)).astype(jnp.bfloat16)
    grad_down = jnp.dot(out_grad.T, activated, preferred_element_type=jnp.float32)
    grad_up = jnp.dot(slot_rows.T, pre_grad, preferred_element_type=jnp.float32)
    input_rows = jnp.dot(pre_grad, slab_up.T, preferred_element_type=jnp.float32).astype(jnp.bfloat16)
    return (expert_out, input_rows, jnp.stack([grad_up, grad_down]))

def group_pass(running, group_data):
    group_tokens, group_cot, group_gates, group_routes, old_ids, new_ids, group_up, group_down = group_data
    slot_count = N_EXPERT
    capacity = CAP
    sources = first_slots(old_ids, new_ids)
    slab_up = group_up[sources]
    slab_down = group_down[sources]
    targets = jax.vmap(partial(slot_targets, slot_count=slot_count, capacity=capacity))(group_routes)
    filled = jax.vmap(partial(fill_slots, slot_total=slot_count * capacity))(targets)
    occupied = (filled > 0)[:, :, None]
    pair_of = jnp.maximum(filled - 1, 0)
    token_of = pair_of // TOPK
    take_rows = jax.vmap(partial(jnp.take, axis=0))
    slot_rows = jnp.where(occupied, take_rows(group_tokens, token_of), 0).astype(jnp.bfloat16)
    scaled = (group_gates[:, :, :, None] * group_cot[:, :, None, :].astype(jnp.float32)).astype(jnp.bfloat16)
    scaled = scaled.reshape(slot_count, TOK_DEV * TOPK, D)
    grad_rows = jnp.where(occupied, take_rows(scaled, pair_of), 0).astype(jnp.bfloat16)
    slot_rows = slot_rows.reshape(slot_count, slot_count, capacity, D).transpose(1, 0, 2, 3).reshape(slot_count, slot_count * capacity, D)
    grad_rows = grad_rows.reshape(slot_count, slot_count, capacity, D).transpose(1, 0, 2, 3).reshape(slot_count, slot_count * capacity, D)
    expert_out, input_rows, slot_grads = lax.map(expert_apply, (slot_rows, grad_rows, slab_up, slab_down))
    offsets = (jnp.arange(slot_count, dtype=jnp.int32) * capacity)[:, None]
    where_back = targets // capacity * (slot_count * capacity) + offsets + targets % capacity
    picked = expert_out.reshape(-1, D)[where_back].reshape(slot_count, TOK_DEV, TOPK, D).astype(jnp.float32)
    layer_out = lax.optimization_barrier(jnp.sum(group_gates[:, :, :, None] * picked, axis=2)).astype(jnp.bfloat16)
    returned_grad = input_rows.reshape(-1, D)[where_back].reshape(slot_count, TOK_DEV, TOPK, D).astype(jnp.float32)
    token_grad = lax.optimization_barrier(jnp.sum(returned_grad, axis=2)).astype(jnp.bfloat16)
    member = (new_ids[None, :] == jnp.arange(EXPERTS, dtype=jnp.int32)[:, None]).astype(jnp.float32)
    running = running + jnp.einsum('es,scrh->ecrh', member, slot_grads, precision=lax.Precision.HIGHEST)
    return (running, (layer_out, token_grad))

def reference(tokens, cotangent, gates, routes, old_place, new_place, up_weight, down_weight, first_moment, second_moment):
    group_data = (tokens.reshape(N_DP, N_EXPERT, TOK_DEV, D), cotangent.reshape(N_DP, N_EXPERT, TOK_DEV, D), gates.reshape(N_DP, N_EXPERT, TOK_DEV, TOPK), routes.reshape(N_DP, N_EXPERT, TOK_DEV, TOPK), old_place, new_place, up_weight, down_weight)
    initial = jnp.zeros((EXPERTS, 2, D, H), jnp.float32)
    expert_grad, outputs = lax.scan(group_pass, initial, group_data)
    layer_out, token_grad = outputs

    def group_update(update_data):
        old_ids, new_ids, group_first, group_second = update_data
        sources = first_slots(old_ids, new_ids)
        return adam_direction(expert_grad[new_ids], group_first[sources], group_second[sources])
    update_dir = lax.map(group_update, (old_place, new_place, first_moment, second_moment))
    return (layer_out.reshape(TOKENS, D), token_grad.reshape(TOKENS, D), update_dir)
```

```python
import jax
import jax.numpy as jnp
from jax import lax
from jax.sharding import PartitionSpec as P

BETA_ONE = 0.9
BETA_TWO = 0.95
EPSILON = 1e-08
Y_SIZE, CORES, Z_SIZE, X_SIZE = 4, 2, 8, 4
GROUPS = Y_SIZE * CORES
SLOTS = Z_SIZE * X_SIZE
EXPERTS = 16
F32 = jnp.float32
BF16 = jnp.bfloat16


def shift_y(value, by):
    pairs = [
        (g, (g // CORES + by) % Y_SIZE * CORES + g % CORES) for g in range(GROUPS)
    ]
    return lax.ppermute(value, "dp", pairs)


def swap_core(value):
    return lax.ppermute(value, "dp", [(g, g ^ 1) for g in range(GROUPS)])


def shift_z(value, by):
    pairs = [
        (s, (s // X_SIZE + by) % Z_SIZE * X_SIZE + s % X_SIZE) for s in range(SLOTS)
    ]
    return lax.ppermute(value, "expert", pairs)


def shift_x(value, by):
    pairs = [
        (s, s // X_SIZE * X_SIZE + (s % X_SIZE + by) % X_SIZE) for s in range(SLOTS)
    ]
    return lax.ppermute(value, "expert", pairs)


def halves(value, axis):
    middle = value.shape[axis] // 2
    return (
        lax.slice_in_dim(value, 0, middle, axis=axis),
        lax.slice_in_dim(value, middle, value.shape[axis], axis=axis),
    )


def ring_gather(own, shift, size, axis):
    found = {0: own}
    ahead = behind = own
    for step in range(1, size // 2):
        ahead, behind = shift(ahead, -1), shift(behind, 1)
        found[step], found[size - step] = ahead, behind
    first, second = halves(ahead, axis)[0], halves(behind, axis)[1]
    found[size // 2] = jnp.concatenate([shift(first, -1), shift(second, 1)], axis=axis)
    return [found[i] for i in range(size)]


def ring_scatter(block, shift, size, axis):
    first, second = halves(block(size // 2), axis)
    up, down = shift(first.astype(BF16), 1), shift(second.astype(BF16), -1)
    for step in range(size // 2 - 1, 0, -1):
        ahead, behind = block(step), block(size - step)
        if step == size // 2 - 1:
            first, second = halves(ahead, axis)
            ahead = jnp.concatenate([first + up.astype(F32), second], axis=axis)
            first, second = halves(behind, axis)
            behind = jnp.concatenate([first, second + down.astype(F32)], axis=axis)
        else:
            ahead, behind = ahead + up.astype(F32), behind + down.astype(F32)
        up, down = shift(ahead.astype(BF16), 1), shift(behind.astype(BF16), -1)
    return block(0) + up.astype(F32) + down.astype(F32)


def in_order(blocks, position):
    size, rows = len(blocks), blocks[0].shape[0]
    twice = jnp.concatenate(blocks + blocks[:-1], axis=0)
    start = (size - position) % size * rows
    return lax.dynamic_slice_in_dim(twice, start, size * rows, axis=0)


def first_slots(old_ids, wanted):
    slot_total = old_ids.shape[0]
    positions = jnp.arange(slot_total, dtype=jnp.int32)
    matches = old_ids[None, :] == wanted[:, None]
    return jnp.min(jnp.where(matches, positions[None, :], slot_total), axis=1)


def adam_direction(expert_grads, first, second):
    new_first = BETA_ONE * first + (1.0 - BETA_ONE) * expert_grads
    new_second = BETA_TWO * second + (1.0 - BETA_TWO) * expert_grads * expert_grads
    return (new_first / (jnp.sqrt(new_second) + EPSILON)).astype(BF16)


def all_to_all(value, axis_name, axis):
    return lax.all_to_all(
        value, axis_name, split_axis=axis, concat_axis=axis, tiled=True
    )


def to_owners(slabs, group, chosen):
    count, rows, hidden = slabs.shape
    piece = rows // SLOTS // GROUPS
    pieces = slabs.reshape(count, SLOTS, GROUPS, piece, hidden)
    mine = lax.dynamic_index_in_dim(pieces, group, axis=2, keepdims=False)
    got = all_to_all(mine, "expert", 1)
    got = jnp.take(got, chosen, axis=1).reshape(count, GROUPS, 2, piece, hidden)
    got = all_to_all(got, "dp", 1)
    return got.transpose(0, 2, 1, 3, 4).reshape(count, 2, GROUPS * piece, hidden)


def per_device(
    tokens,
    cotangent,
    gates,
    routes,
    old_place,
    new_place,
    up_weight,
    down_weight,
    first_moment,
    second_moment,
):
    token_count, width = tokens.shape
    hidden = up_weight.shape[3]
    rows = 2 * width
    group, slot = lax.axis_index("dp"), lax.axis_index("expert")
    y_at, core_at = group // CORES, group % CORES
    z_at, x_at = slot // X_SIZE, slot % X_SIZE
    old_ids, new_ids = old_place[0], new_place[0]
    chosen = first_slots(old_ids, jnp.arange(EXPERTS, dtype=jnp.int32))

    slab = jnp.concatenate([up_weight[0, 0], down_weight[0, 0]], axis=0)
    shard = to_owners(slab[None], group, chosen)[0]
    along_x = ring_gather(shard[0], shift_x, X_SIZE, 0)
    along_z = ring_gather(in_order(along_x, x_at), shift_z, Z_SIZE, 0)
    left = in_order(along_z, z_at)
    along_z = ring_gather(shard[1], shift_z, Z_SIZE, 0)
    column = jnp.stack(along_z)
    along_x = ring_gather(column, shift_x, X_SIZE, 0)
    right = in_order([b[None] for b in along_x], x_at)
    right = right.transpose(1, 0, 2, 3)
    right = in_order([right[i] for i in range(Z_SIZE)], z_at).reshape(rows, hidden)
    weights = jnp.concatenate([left, right], axis=1)
    up, down = weights[:width], weights[width:]

    expert_of = jnp.sum(
        jnp.where(
            routes[:, :, None] == jnp.arange(SLOTS, dtype=jnp.int32), new_ids, 0
        ),
        axis=2,
    )
    of_expert = expert_of[None] == jnp.arange(EXPERTS, dtype=jnp.int32)[:, None, None]
    gate_sums = jnp.sum(jnp.where(of_expert, gates[None], 0.0), axis=2)
    own = jnp.stack([tokens, cotangent])
    near = jnp.stack(ring_gather(own, shift_y, Y_SIZE, 1))
    far = swap_core(near)
    near_gates = jnp.stack(ring_gather(gate_sums, shift_y, Y_SIZE, 1))
    far_gates = swap_core(near_gates)
    everyone = jnp.concatenate([near, far], axis=0)
    x_rows = everyone[:, 0].reshape(GROUPS * token_count, width)
    c_rows = everyone[:, 1].reshape(GROUPS * token_count, width)
    all_gates = jnp.concatenate([near_gates, far_gates], axis=0)
    mine = lax.dynamic_slice_in_dim(all_gates, 2 * group, 2, axis=1)
    scale = mine.transpose(0, 2, 1).reshape(GROUPS * token_count, 2)
    scale = jnp.repeat(scale, hidden, axis=1)

    pre = jnp.dot(x_rows, up, preferred_element_type=F32)
    hidden_grad = jnp.dot(c_rows, down, preferred_element_type=F32)
    sigmoid = jax.nn.sigmoid(pre)
    act = (pre * sigmoid).astype(BF16).astype(F32)
    act = (act * scale).astype(BF16)
    slope = sigmoid * (1.0 + pre * (1.0 - sigmoid))
    pgrad = (hidden_grad * scale * slope).astype(BF16)
    grads = jnp.concatenate(
        [
            lax.dot_general(x_rows, pgrad, (((0,), (0,)), ((), ())), preferred_element_type=F32),
            lax.dot_general(c_rows, act, (((0,), (0,)), ((), ())), preferred_element_type=F32),
        ],
        axis=0,
    )
    contract = (((1,), (1,)), ((), ()))
    out_part = lax.dot_general(act, down, contract, preferred_element_type=F32)
    back_part = lax.dot_general(pgrad, up, contract, preferred_element_type=F32)

    table = grads.reshape(Z_SIZE, X_SIZE, rows // SLOTS, 2, hidden)
    table_left, table_right = table[:, :, :, 0], table[:, :, :, 1]

    def left_x(distance):
        return lax.dynamic_index_in_dim(
            table_left, (x_at + distance) % X_SIZE, axis=1, keepdims=False
        )

    column = ring_scatter(left_x, shift_x, X_SIZE, 0)
    sum_left = ring_scatter(
        lambda distance: lax.dynamic_index_in_dim(
            column, (z_at + distance) % Z_SIZE, axis=0, keepdims=False
        ),
        shift_z,
        Z_SIZE,
        0,
    )

    def right_z(distance):
        return lax.dynamic_index_in_dim(
            table_right, (z_at + distance) % Z_SIZE, axis=0, keepdims=False
        )

    line = ring_scatter(right_z, shift_z, Z_SIZE, 0)
    sum_right = ring_scatter(
        lambda distance: lax.dynamic_index_in_dim(
            line, (x_at + distance) % X_SIZE, axis=0, keepdims=False
        ),
        shift_x,
        X_SIZE,
        0,
    )

    parts = jnp.stack([out_part, back_part]).reshape(2, CORES, Y_SIZE, token_count, width)
    met = parts[:, 0] + swap_core(parts[:, 1].astype(BF16)).astype(F32)
    token_sums = ring_scatter(lambda distance: met[:, distance], shift_y, Y_SIZE, 1)
    token_sums = token_sums.astype(BF16)

    moments = jnp.stack(
        [first_moment.reshape(rows, hidden), second_moment.reshape(rows, hidden)]
    )
    moments = to_owners(moments, group, chosen)
    update = adam_direction(jnp.stack([sum_left, sum_right]), moments[0], moments[1])
    near = jnp.stack(ring_gather(update, shift_y, Y_SIZE, 1))
    table = jnp.concatenate([near, swap_core(near)], axis=0)
    table = table.reshape(EXPERTS, rows // SLOTS, hidden)
    owner = new_ids // 2
    at = (owner % CORES ^ core_at) * Y_SIZE + (owner // CORES - y_at) % Y_SIZE
    sent = jnp.take(table, at * 2 + new_ids % 2, axis=0)
    final = all_to_all(sent, "expert", 0)
    return (token_sums[0], token_sums[1], final.reshape(1, 1, 2, width, hidden))


def solution(mesh):
    by_token = P(("dp", "expert"), None)
    by_group = P("dp", None)
    by_slot = P("dp", "expert", None, None)
    by_slot_pair = P("dp", "expert", None, None, None)
    return jax.shard_map(
        per_device,
        mesh=mesh,
        in_specs=(
            by_token,
            by_token,
            by_token,
            by_token,
            by_group,
            by_group,
            by_slot,
            by_slot,
            by_slot_pair,
            by_slot_pair,
        ),
        out_specs=(by_token, by_token, by_slot_pair),
        check_vma=False,
    )
```
